32 devices in a mesh: ops: 4 (over y, x), blk: 8 (over z, core).
Axes of the slice: x: 2, y: 2, z: 4, core: 2. Of those that a mesh axis runs over, the one named last changes fastest.
Arguments:
- psi: bfloat16 [2048, 1024], P('blk'), may hold values from -6 to 6
- left_env: bfloat16 [16, 8, 256, 256], P('ops', 'blk'), may hold values from -0.09375 to 0.09375
- right_env: bfloat16 [16, 8, 128, 128], P('ops', 'blk'), may hold values from -0.5 to 0.5
- left_live: int32 [8], replicated, may hold values from 64 to 256, as said below
- right_live: int32 [8], replicated, may hold values from 32 to 128, as said below
Outputs:
- hpsi: float32 [2048, 1024], P('blk', 'ops')
The draws below stay inside these ranges and needn't reach their ends.
Inputs may be any that keep to these rules, and one draw needn't show every extreme that they name: `left_live`: some left sector is fully live. `right_live`: some right sector is fully live.
All inputs are finite; a program needn't handle non-finite values.
Results may differ from the reference program's by a relative error of at most 0.0029.
Values may be sent and summed in bfloat16 or wider, within the bound.
A program may use at most 128 MiB of HBM per device.

```python
import jax
import jax.numpy as jnp
from jax import lax

PL = 256
PR = 128
TERMS = 16
SECTORS = 8


def draw_left_live(key, part):
    values = jax.random.randint(key, (SECTORS,), PL // 4, PL + 1)
    where_full = jax.random.randint(jax.random.fold_in(key, 11), (), 0, SECTORS)
    return values.at[where_full].set(PL).astype(jnp.int32)


def draw_right_live(key, part):
    inner = jax.random.fold_in(key, 23)
    values = jax.random.randint(inner, (SECTORS,), PR // 4, PR + 1)
    where_full = jax.random.randint(jax.random.fold_in(key, 29), (), 0, SECTORS)
    return values.at[where_full].set(PR).astype(jnp.int32)


def shard_levels(rng, extent, shards, least, top_value):
    def one(dim, blocks):
        heights = jax.random.uniform(jax.random.fold_in(jax.random.fold_in(rng, 6), dim), (blocks,), jnp.float32, least / len(shards), top_value / len(shards))
        return jnp.repeat(jnp.exp(heights), extent[dim] // blocks).reshape((-1,) + (1,) * (len(extent) - dim - 1))

    gain = one(*shards[0])
    for cut in shards[1:]:
        gain = gain * one(*cut)
    return gain


def noise(key, extent, spread, limit, split=(), kind=jnp.bfloat16):
    drawn = spread * jax.random.normal(key, extent, jnp.float32)
    if split:
        drawn = drawn * shard_levels(key, extent, split, -0.22, 0.18)
    return jnp.clip(drawn, -limit, limit).astype(kind)


def setup_inputs(seed: int = 0) -> dict:
    streams_of = jax.random.split(jax.random.key(seed), 6)
    psi = noise(streams_of[0], (SECTORS * PL, SECTORS * PR), 1.0, 6.0, ((0, 8),))
    left_env = noise(streams_of[1], (TERMS, SECTORS, PL, PL), (PL * TERMS) ** -0.5, 0.09375, ((0, 4), (1, 8)))
    right_env = noise(streams_of[2], (TERMS, SECTORS, PR, PR), PR ** -0.5, 0.5, ((0, 4), (1, 8)))
    left_live = draw_left_live(jax.random.fold_in(streams_of[5], 71), 0)
    right_live = draw_right_live(jax.random.fold_in(streams_of[5], 71), 0)
    return {"psi": psi, "left_env": left_env, "right_env": right_env, "left_live": left_live, "right_live": right_live}


def reference(psi, left_env, right_env, left_live, right_live):
    sectors = left_live.shape[0]
    pl = left_env.shape[2]
    pr = right_env.shape[2]
    row_mask = (jnp.arange(pl, dtype=jnp.int32)[None, :] < left_live[:, None]).reshape(sectors * pl)
    col_mask = (jnp.arange(pr, dtype=jnp.int32)[None, :] < right_live[:, None]).reshape(sectors * pr)
    mask = row_mask[:, None] & col_mask[None, :]
    masked = jnp.where(mask, psi, jnp.zeros_like(psi)).astype(jnp.float32).reshape(sectors, pl, sectors, pr)

    def one_term(acc, envs):
        left_w, right_w = envs
        mixed = jnp.einsum('iab,ibjr->iajr', left_w.astype(jnp.float32), masked).astype(jnp.bfloat16)
        mixed = lax.optimization_barrier(mixed).astype(jnp.float32)
        return acc + jnp.einsum('iajr,jsr->iajs', mixed, right_w.astype(jnp.float32)), None

    start = jnp.zeros((sectors, pl, sectors, pr), jnp.float32)
    total, unused = lax.scan(one_term, start, (left_env, right_env))
    total = total.reshape(sectors * pl, sectors * pr)
    return jnp.where(mask, total, jnp.zeros_like(total))
```

```python
import functools

import jax
import jax.numpy as jnp
from jax import lax
from jax.experimental import pallas as pl
from jax.experimental.pallas import tpu as pltpu
from jax.sharding import PartitionSpec as P

MESH = pl.DeviceIdType.MESH
CHUNKS = 2


def kernel(
    groups, sectors, left_live, right_live, psi, left, right, out,
    psi_v, left_v, mixed, rights, sent, landed, own,
    local_sem, env_send, env_recv, sum_send, sum_recv,
):
    terms, size, width = left.shape[0], left.shape[2], right.shape[2]
    share = sectors // groups
    chips = sectors // 2
    part = terms // CHUNKS
    group, me = lax.axis_index("ops"), lax.axis_index("blk")
    chip, core = me // 2, me % 2
    sister = 2 * chip + 1 - core
    has_prev, has_next = chip > 0, chip < chips - 1

    load_psi = pltpu.make_async_copy(psi, psi_v, local_sem.at[0])
    load_left = pltpu.make_async_copy(left.at[:, 0], left_v, local_sem.at[1])
    load_right = pltpu.make_async_copy(right.at[:, 0], rights.at[me], local_sem.at[2])
    load_psi.start()
    load_left.start()
    load_right.start()

    barrier = pltpu.get_barrier_semaphore()

    def greet(where):
        pl.semaphore_signal(barrier, inc=1, device_id=where, device_id_type=MESH)

    greet({"blk": sister})
    pl.when(has_prev)(lambda: greet({"blk": me - 2}))
    pl.when(has_next)(lambda: greet({"blk": me + 2}))
    for step in range(1, groups):
        greet({"ops": (group + step) % groups})
    pl.semaphore_wait(barrier, groups + has_prev.astype(jnp.int32) + has_next.astype(jnp.int32))

    def pieces(k):
        return pl.ds(k * part, part)

    def env_copy(sector, k, way, target, source=None):
        landing = rights.at[sector, pieces(k)]
        return pltpu.make_async_remote_copy(
            src_ref=landing if source is None else source,
            dst_ref=landing,
            send_sem=env_send.at[sector, way, k],
            recv_sem=env_recv.at[sector, k],
            device_id={"blk": target},
            device_id_type=MESH,
        )

    def own_copy(k, way, target):
        return env_copy(me, k, way, target, right.at[pieces(k), 0])

    for k in range(CHUNKS):
        pl.when(has_next)(lambda: own_copy(k, 1, me + 2).start())
        pl.when(has_prev)(lambda: own_copy(k, 2, me - 2).start())
        own_copy(k, 0, sister).start()

    row = lax.broadcasted_iota(jnp.int32, (size, width), 0)
    lane = lax.broadcasted_iota(jnp.int32, (size, width), 1)
    row_live = row < left_live[me]

    load_psi.wait()
    load_left.wait()
    stacked = left_v[...].reshape(terms * size, size)

    def mix(pair, carry):
        blocks = []
        for half in range(2):
            sector = 2 * pair + half
            block = psi_v[:, pl.ds(pl.multiple_of(sector * width, width), width)].astype(jnp.float32)
            live = row_live & (lane < right_live[sector])
            blocks.append(jnp.where(live, block, 0.0).astype(jnp.bfloat16))
        both = jnp.dot(stacked, jnp.concatenate(blocks, axis=1), preferred_element_type=jnp.float32)
        both = both.astype(jnp.bfloat16)
        for half in range(2):
            mixed[2 * pair + half] = both[:, half * width:(half + 1) * width].reshape(terms, size, width)
        return carry

    lax.fori_loop(0, chips, mix, 0)

    def sum_copy(sector):
        return pltpu.make_async_remote_copy(
            src_ref=sent.at[sector],
            dst_ref=landed.at[group, sector % share],
            send_sem=sum_send.at[sector],
            recv_sem=sum_recv.at[group, sector % share],
            device_id={"ops": sector // share},
            device_id_type=MESH,
        )

    def finish(sector):
        lhs = jnp.concatenate([mixed[sector, w] for w in range(terms)], axis=1)
        rhs = jnp.concatenate([rights[sector, w] for w in range(terms)], axis=1)
        value = lax.dot_general(lhs, rhs, (((1,), (1,)), ((), ())), preferred_element_type=jnp.float32)
        mine = sector // share == group

        @pl.when(mine)
        def _():
            own[sector % share] = value

        @pl.when(jnp.logical_not(mine))
        def _():
            sent[sector] = value.astype(sent.dtype)
            sum_copy(sector).start()

    def arrive(sector):
        for k in range(CHUNKS):
            env_copy(sector, k, 0, sister).wait_recv()

    load_right.wait()
    finish(me)
    arrive(sister)
    finish(sister)

    def step(distance, carry):
        before, after = chip - distance >= 0, chip + distance < chips
        low, high = me - 2 * distance, me + 2 * distance
        for k in range(CHUNKS):
            @pl.when(before)
            def _():
                env_copy(low, k, 0, sister).wait_recv()
                pl.when(has_next)(lambda: env_copy(low, k, 1, me + 2).start())
                env_copy(low, k, 0, sister).start()

            @pl.when(after)
            def _():
                env_copy(high, k, 0, sister).wait_recv()
                pl.when(has_prev)(lambda: env_copy(high, k, 2, me - 2).start())
                env_copy(high, k, 0, sister).start()

        pl.when(before)(lambda: finish(low))
        pl.when(after)(lambda: finish(high))

        @pl.when(before)
        def _():
            arrive(sister - 2 * distance)
            finish(sister - 2 * distance)

        @pl.when(after)
        def _():
            arrive(sister + 2 * distance)
            finish(sister + 2 * distance)

        return carry

    lax.fori_loop(1, chips, step, 0)

    def gather(slot, carry):
        total = own[slot]
        for turn in range(1, groups):
            source = (group + turn) % groups
            pltpu.make_async_remote_copy(
                src_ref=sent.at[slot],
                dst_ref=landed.at[source, slot],
                send_sem=sum_send.at[slot],
                recv_sem=sum_recv.at[source, slot],
                device_id={"ops": source},
                device_id_type=MESH,
            ).wait_recv()
            total = total + landed[source, slot].astype(jnp.float32)
        live = row_live & (lane < right_live[group * share + slot])
        out[:, pl.ds(pl.multiple_of(slot * width, width), width)] = jnp.where(live, total, 0.0)
        return carry

    lax.fori_loop(0, share, gather, 0)

    for k in range(CHUNKS):
        pl.when(has_next)(lambda: own_copy(k, 1, me + 2).wait_send())
        pl.when(has_prev)(lambda: own_copy(k, 2, me - 2).wait_send())
        own_copy(k, 0, sister).wait_send()

    def drain_env(distance, carry):
        low, high = me - 2 * distance, me + 2 * distance

        @pl.when(low >= 0)
        def _():
            for k in range(CHUNKS):
                pl.when(has_next)(lambda: env_copy(low, k, 1, me + 2).wait_send())
                env_copy(low, k, 0, sister).wait_send()

        @pl.when(high < sectors)
        def _():
            for k in range(CHUNKS):
                pl.when(has_prev)(lambda: env_copy(high, k, 2, me - 2).wait_send())
                env_copy(high, k, 0, sister).wait_send()

        return carry

    lax.fori_loop(1, chips, drain_env, 0)

    def drain_sums(sector, carry):
        pl.when(sector // share != group)(lambda: sum_copy(sector).wait_send())
        return carry

    lax.fori_loop(0, sectors, drain_sums, 0)


def shards(psi, left_env, right_env, left_live, right_live):
    groups, sectors = lax.axis_size("ops"), lax.axis_size("blk")
    terms, size, width = left_env.shape[0], left_env.shape[2], right_env.shape[2]
    share = sectors // groups
    bf16, f32 = jnp.bfloat16, jnp.float32
    buffers = [
        ((size, sectors * width), bf16),
        ((terms, size, size), bf16),
        ((sectors, terms, size, width), bf16),
        ((sectors, terms, width, width), bf16),
        ((sectors, size, width), bf16),
        ((groups, share, size, width), bf16),
        ((share, size, width), f32),
    ]
    held = sum(int(jnp.dtype(kind).itemsize) * functools.reduce(int.__mul__, shape) for shape, kind in buffers)
    dma = pltpu.SemaphoreType.DMA
    return pl.pallas_call(
        functools.partial(kernel, groups, sectors),
        out_shape=jax.ShapeDtypeStruct((size, share * width), f32),
        in_specs=[pl.BlockSpec(memory_space=pltpu.SMEM)] * 2 + [pl.BlockSpec(memory_space=pl.ANY)] * 3,
        out_specs=pl.BlockSpec(memory_space=pltpu.VMEM),
        scratch_shapes=[pltpu.VMEM(shape, kind) for shape, kind in buffers] + [
            dma((3,)),
            dma((sectors, 3, CHUNKS)),
            dma((sectors, CHUNKS)),
            dma((sectors,)),
            dma((groups, share)),
        ],
        compiler_params=pltpu.CompilerParams(
            collective_id=0, has_side_effects=True,
            vmem_limit_bytes=held + 2 * 4 * size * share * width + (10 << 20),
        ),
    )(left_live, right_live, psi, left_env, right_env)


def solution(mesh):
    in_specs = (P("blk", None), P("ops", "blk", None, None), P("ops", "blk", None, None), P(), P())
    out_specs = P("blk", "ops")
    return jax.shard_map(shards, mesh=mesh, in_specs=in_specs, out_specs=out_specs, check_vma=False)
```

```python
import functools

import jax
import jax.numpy as jnp
from jax import lax
from jax.experimental import pallas as pl
from jax.experimental.pallas import tpu as pltpu
from jax.sharding import PartitionSpec as P

MESH = pl.DeviceIdType.MESH
CHUNKS = 2
VMEM = 60 << 20


def kernel(
    groups, sectors, left_hbm, right_hbm, psi, left, right, out,
    left_live, right_live, psi_v, left_v, mixed, rights, sent, landed, own,
    local_sem, env_send, env_recv, sum_send, sum_recv,
):
    terms, size, width = left.shape[0], left.shape[2], right.shape[2]
    share = sectors // groups
    chips = sectors // 2
    part = terms // CHUNKS
    group, me = lax.axis_index("ops"), lax.axis_index("blk")
    chip, core = me // 2, me % 2
    sister = 2 * chip + 1 - core
    has_prev, has_next = chip > 0, chip < chips - 1

    load_psi = pltpu.make_async_copy(psi, psi_v, local_sem.at[0])
    load_left = pltpu.make_async_copy(left.at[:, 0], left_v, local_sem.at[1])
    load_right = pltpu.make_async_copy(right.at[:, 0], rights.at[me], local_sem.at[2])
    load_left_live = pltpu.make_async_copy(left_hbm, left_live, local_sem.at[3])
    load_right_live = pltpu.make_async_copy(right_hbm, right_live, local_sem.at[4])
    load_left_live.start()
    load_right_live.start()
    load_psi.start()
    load_left.start()
    load_right.start()

    barrier = pltpu.get_barrier_semaphore()

    def greet(where):
        pl.semaphore_signal(barrier, inc=1, device_id=where, device_id_type=MESH)

    greet({"blk": sister})
    pl.when(has_prev)(lambda: greet({"blk": me - 2}))
    pl.when(has_next)(lambda: greet({"blk": me + 2}))
    for step in range(1, groups):
        greet({"ops": (group + step) % groups})
    pl.semaphore_wait(barrier, groups + has_prev.astype(jnp.int32) + has_next.astype(jnp.int32))

    def pieces(k):
        return pl.ds(k * part, part)

    def env_copy(sector, k, way, target, source=None):
        landing = rights.at[sector, pieces(k)]
        return pltpu.make_async_remote_copy(
            src_ref=landing if source is None else source,
            dst_ref=landing,
            send_sem=env_send.at[sector, way, k],
            recv_sem=env_recv.at[sector, k],
            device_id={"blk": target},
            device_id_type=MESH,
        )

    def own_copy(k, way, target):
        return env_copy(me, k, way, target, right.at[pieces(k), 0])

    for k in range(CHUNKS):
        pl.when(has_next)(lambda: own_copy(k, 1, me + 2).start())
        pl.when(has_prev)(lambda: own_copy(k, 2, me - 2).start())
        own_copy(k, 0, sister).start()

    row = lax.broadcasted_iota(jnp.int32, (size, width), 0)
    lane = lax.broadcasted_iota(jnp.int32, (size, width), 1)
    load_left_live.wait()
    load_right_live.wait()
    row_live = row < left_live[me]

    load_psi.wait()
    load_left.wait()
    stacked = left_v[...].reshape(terms * size, size)

    def mix(pair, carry):
        blocks = []
        for half in range(2):
            sector = 2 * pair + half
            block = psi_v[:, pl.ds(pl.multiple_of(sector * width, width), width)].astype(jnp.float32)
            live = row_live & (lane < right_live[sector])
            blocks.append(jnp.where(live, block, 0.0).astype(jnp.bfloat16))
        both = jnp.dot(stacked, jnp.concatenate(blocks, axis=1), preferred_element_type=jnp.float32)
        both = both.astype(jnp.bfloat16)
        for half in range(2):
            mixed[2 * pair + half] = both[:, half * width:(half + 1) * width].reshape(terms, size, width)
        return carry

    lax.fori_loop(0, chips, mix, 0)

    def sum_copy(sector):
        return pltpu.make_async_remote_copy(
            src_ref=sent.at[sector],
            dst_ref=landed.at[group, sector % share],
            send_sem=sum_send.at[sector],
            recv_sem=sum_recv.at[group, sector % share],
            device_id={"ops": sector // share},
            device_id_type=MESH,
        )

    def finish(sector):
        lhs = jnp.concatenate([mixed[sector, w] for w in range(terms)], axis=1)
        rhs = jnp.concatenate([rights[sector, w] for w in range(terms)], axis=1)
        value = lax.dot_general(lhs, rhs, (((1,), (1,)), ((), ())), preferred_element_type=jnp.float32)
        mine = sector // share == group

        @pl.when(mine)
        def _():
            own[sector % share] = value

        @pl.when(jnp.logical_not(mine))
        def _():
            sent[sector] = value.astype(sent.dtype)
            sum_copy(sector).start()

    def arrive(sector):
        for k in range(CHUNKS):
            env_copy(sector, k, 0, sister).wait_recv()

    def relay(distance, k):
        low, high = me - 2 * distance, me + 2 * distance

        @pl.when(low >= 0)
        def _():
            env_copy(low, k, 0, sister).wait_recv()
            pl.when(has_next)(lambda: env_copy(low, k, 1, me + 2).start())
            env_copy(low, k, 0, sister).start()

        @pl.when(high < sectors)
        def _():
            env_copy(high, k, 0, sister).wait_recv()
            pl.when(has_prev)(lambda: env_copy(high, k, 2, me - 2).start())
            env_copy(high, k, 0, sister).start()

    def finish_sister(sector):
        arrive(sector)
        finish(sector)

    load_right.wait()

    def step(distance, carry):
        behind = distance - 1
        low, high = me - 2 * behind, me + 2 * behind
        below, above = low >= 0, (high < sectors) & (behind > 0)
        relay(distance, 0)
        pl.when(below)(lambda: finish(low))
        pl.when(above)(lambda: finish(high))
        for k in range(1, CHUNKS):
            relay(distance, k)
        pl.when(below)(lambda: finish_sister(sister - 2 * behind))
        pl.when(above)(lambda: finish_sister(sister + 2 * behind))
        return carry

    lax.fori_loop(1, chips + 1, step, 0)

    def gather(slot, carry):
        total = own[slot]
        for turn in range(1, groups):
            source = (group + turn) % groups
            pltpu.make_async_remote_copy(
                src_ref=sent.at[slot],
                dst_ref=landed.at[source, slot],
                send_sem=sum_send.at[slot],
                recv_sem=sum_recv.at[source, slot],
                device_id={"ops": source},
                device_id_type=MESH,
            ).wait_recv()
            total = total + landed[source, slot].astype(jnp.float32)
        live = row_live & (lane < right_live[group * share + slot])
        out[:, pl.ds(pl.multiple_of(slot * width, width), width)] = jnp.where(live, total, 0.0)
        return carry

    lax.fori_loop(0, share, gather, 0)

    for k in range(CHUNKS):
        pl.when(has_next)(lambda: own_copy(k, 1, me + 2).wait_send())
        pl.when(has_prev)(lambda: own_copy(k, 2, me - 2).wait_send())
        own_copy(k, 0, sister).wait_send()

    def drain_env(distance, carry):
        low, high = me - 2 * distance, me + 2 * distance

        @pl.when(low >= 0)
        def _():
            for k in range(CHUNKS):
                pl.when(has_next)(lambda: env_copy(low, k, 1, me + 2).wait_send())
                env_copy(low, k, 0, sister).wait_send()

        @pl.when(high < sectors)
        def _():
            for k in range(CHUNKS):
                pl.when(has_prev)(lambda: env_copy(high, k, 2, me - 2).wait_send())
                env_copy(high, k, 0, sister).wait_send()

        return carry

    lax.fori_loop(1, chips, drain_env, 0)

    def drain_sums(sector, carry):
        pl.when(sector // share != group)(lambda: sum_copy(sector).wait_send())
        return carry

    lax.fori_loop(0, sectors, drain_sums, 0)


def shards(psi, left_env, right_env, left_live, right_live):
    groups, sectors = lax.axis_size("ops"), lax.axis_size("blk")
    terms, size, width = left_env.shape[0], left_env.shape[2], right_env.shape[2]
    share = sectors // groups
    bf16, f32 = jnp.bfloat16, jnp.float32
    buffers = [
        ((size, sectors * width), bf16),
        ((terms, size, size), bf16),
        ((sectors, terms, size, width), bf16),
        ((sectors, terms, width, width), bf16),
        ((sectors, size, width), bf16),
        ((groups, share, size, width), bf16),
        ((share, size, width), f32),
    ]
    dma = pltpu.SemaphoreType.DMA
    return pl.pallas_call(
        functools.partial(kernel, groups, sectors),
        out_shape=jax.ShapeDtypeStruct((size, share * width), f32),
        in_specs=[pl.BlockSpec(memory_space=pltpu.HBM)] * 5,
        out_specs=pl.BlockSpec(memory_space=pltpu.VMEM),
        scratch_shapes=[pltpu.SMEM((sectors,), jnp.int32)] * 2 + [pltpu.VMEM(shape, kind) for shape, kind in buffers] + [
            dma((5,)),
            dma((sectors, 3, CHUNKS)),
            dma((sectors, CHUNKS)),
            dma((sectors,)),
            dma((groups, share)),
        ],
        compiler_params=pltpu.CompilerParams(
            collective_id=0, has_side_effects=True,
            vmem_limit_bytes=VMEM,
        ),
    )(left_live, right_live, psi, left_env, right_env)


def solution(mesh):
    in_specs = (P("blk", None), P("ops", "blk", None, None), P("ops", "blk", None, None), P(), P())
    out_specs = P("blk", "ops")
    return jax.shard_map(shards, mesh=mesh, in_specs=in_specs, out_specs=out_specs, check_vma=False)
```

```python
import functools

import jax
import jax.numpy as jnp
from jax import lax
from jax.experimental import pallas as pl
from jax.experimental.pallas import tpu as pltpu
from jax.sharding import PartitionSpec as P

MESH = pl.DeviceIdType.MESH
CHUNKS = 2
VMEM = 60 << 20


def kernel(
    groups, sectors, left_hbm, right_hbm, psi, left, right, out,
    left_live, right_live, psi_v, left_v, mixed, rights, sent, landed, own,
    local_sem, env_send, env_recv, sum_send, sum_recv,
):
    terms, size, width = left.shape[0], left.shape[2], right.shape[2]
    share = sectors // groups
    chips = sectors // 2
    part = terms // CHUNKS
    group, me = lax.axis_index("ops"), lax.axis_index("blk")
    chip, core = me // 2, me % 2
    sister = 2 * chip + 1 - core
    has_prev, has_next = chip > 0, chip < chips - 1
    has_prev2, has_next2 = chip > 1, chip < chips - 2

    load_psi = pltpu.make_async_copy(psi, psi_v, local_sem.at[0])
    load_left = pltpu.make_async_copy(left.at[:, 0], left_v, local_sem.at[1])
    load_right = pltpu.make_async_copy(right.at[:, 0], rights.at[me], local_sem.at[2])
    load_left_live = pltpu.make_async_copy(left_hbm, left_live, local_sem.at[3])
    load_right_live = pltpu.make_async_copy(right_hbm, right_live, local_sem.at[4])
    load_left_live.start()
    load_right_live.start()
    load_psi.start()
    load_left.start()
    load_right.start()

    barrier = pltpu.get_barrier_semaphore()

    def greet(where):
        pl.semaphore_signal(barrier, inc=1, device_id=where, device_id_type=MESH)

    greet({"blk": sister})
    pl.when(has_prev)(lambda: greet({"blk": me - 2}))
    pl.when(has_next)(lambda: greet({"blk": me + 2}))
    pl.when(has_prev2)(lambda: greet({"blk": me - 4}))
    pl.when(has_next2)(lambda: greet({"blk": me + 4}))
    for step in range(1, groups):
        greet({"ops": (group + step) % groups})
    near = sum(there.astype(jnp.int32) for there in (has_prev, has_next, has_prev2, has_next2))
    pl.semaphore_wait(barrier, groups + near)

    def pieces(k):
        return pl.ds(k * part, part)

    def env_copy(sector, k, way, target, source=None):
        landing = rights.at[sector, pieces(k)]
        return pltpu.make_async_remote_copy(
            src_ref=landing if source is None else source,
            dst_ref=landing,
            send_sem=env_send.at[sector, way, k],
            recv_sem=env_recv.at[sector, k],
            device_id={"blk": target},
            device_id_type=MESH,
        )

    def upward(use, sector, k, source=None):
        pl.when(has_next2)(lambda: use(env_copy(sector, k, 3, me + 4, source)))
        pl.when(has_next)(lambda: use(env_copy(sector, k, 1, me + 2, source)))

    def downward(use, sector, k, source=None):
        pl.when(has_prev2)(lambda: use(env_copy(sector, k, 4, me - 4, source)))
        pl.when(has_prev)(lambda: use(env_copy(sector, k, 2, me - 2, source)))

    def start(copy):
        copy.start()

    def sent_off(copy):
        copy.wait_send()

    for k in range(CHUNKS):
        source = right.at[pieces(k), 0]
        upward(start, me, k, source)
        downward(start, me, k, source)
        env_copy(me, k, 0, sister, source).start()

    row = lax.broadcasted_iota(jnp.int32, (size, width), 0)
    lane = lax.broadcasted_iota(jnp.int32, (size, width), 1)
    load_left_live.wait()
    load_right_live.wait()
    row_live = row < left_live[me]

    load_psi.wait()
    load_left.wait()
    stacked = left_v[...].reshape(terms * size, size)

    def mix(pair, carry):
        blocks = []
        for half in range(2):
            sector = 2 * pair + half
            block = psi_v[:, pl.ds(pl.multiple_of(sector * width, width), width)].astype(jnp.float32)
            live = row_live & (lane < right_live[sector])
            blocks.append(jnp.where(live, block, 0.0).astype(jnp.bfloat16))
        both = jnp.dot(stacked, jnp.concatenate(blocks, axis=1), preferred_element_type=jnp.float32)
        both = both.astype(jnp.bfloat16)
        for half in range(2):
            mixed[2 * pair + half] = both[:, half * width:(half + 1) * width].reshape(terms, size, width)
        return carry

    lax.fori_loop(0, chips, mix, 0)

    def sum_copy(sector):
        return pltpu.make_async_remote_copy(
            src_ref=sent.at[sector],
            dst_ref=landed.at[group, sector % share],
            send_sem=sum_send.at[sector],
            recv_sem=sum_recv.at[group, sector % share],
            device_id={"ops": sector // share},
            device_id_type=MESH,
        )

    def finish(sector):
        lhs = jnp.concatenate([mixed[sector, w] for w in range(terms)], axis=1)
        rhs = jnp.concatenate([rights[sector, w] for w in range(terms)], axis=1)
        value = lax.dot_general(lhs, rhs, (((1,), (1,)), ((), ())), preferred_element_type=jnp.float32)
        mine = sector // share == group

        @pl.when(mine)
        def _():
            own[sector % share] = value

        @pl.when(jnp.logical_not(mine))
        def _():
            sent[sector] = value.astype(sent.dtype)
            sum_copy(sector).start()

    def arrive(sector):
        for k in range(CHUNKS):
            env_copy(sector, k, 0, sister).wait_recv()

    def relay(distance, k):
        low, high = me - 2 * distance, me + 2 * distance
        even = distance % 2 == 0

        @pl.when(low >= 0)
        def _():
            env_copy(low, k, 0, sister).wait_recv()
            pl.when(even)(lambda: upward(start, low, k))
            env_copy(low, k, 0, sister).start()

        @pl.when(high < sectors)
        def _():
            env_copy(high, k, 0, sister).wait_recv()
            pl.when(even)(lambda: downward(start, high, k))
            env_copy(high, k, 0, sister).start()

    def finish_sister(sector):
        arrive(sector)
        finish(sector)

    load_right.wait()

    def step(distance, carry):
        behind = distance - 1
        low, high = me - 2 * behind, me + 2 * behind
        below, above = low >= 0, (high < sectors) & (behind > 0)
        relay(distance, 0)
        pl.when(below)(lambda: finish(low))
        pl.when(above)(lambda: finish(high))
        for k in range(1, CHUNKS):
            relay(distance, k)
        pl.when(below)(lambda: finish_sister(sister - 2 * behind))
        pl.when(above)(lambda: finish_sister(sister + 2 * behind))
        return carry

    lax.fori_loop(1, chips + 1, step, 0)

    def gather(slot, carry):
        total = own[slot]
        for turn in range(1, groups):
            source = (group + turn) % groups
            pltpu.make_async_remote_copy(
                src_ref=sent.at[slot],
                dst_ref=landed.at[source, slot],
                send_sem=sum_send.at[slot],
                recv_sem=sum_recv.at[source, slot],
                device_id={"ops": source},
                device_id_type=MESH,
            ).wait_recv()
            total = total + landed[source, slot].astype(jnp.float32)
        live = row_live & (lane < right_live[group * share + slot])
        out[:, pl.ds(pl.multiple_of(slot * width, width), width)] = jnp.where(live, total, 0.0)
        return carry

    lax.fori_loop(0, share, gather, 0)

    for k in range(CHUNKS):
        source = right.at[pieces(k), 0]
        upward(sent_off, me, k, source)
        downward(sent_off, me, k, source)
        env_copy(me, k, 0, sister, source).wait_send()

    def drain_env(distance, carry):
        low, high = me - 2 * distance, me + 2 * distance
        even = distance % 2 == 0

        @pl.when(low >= 0)
        def _():
            for k in range(CHUNKS):
                pl.when(even)(lambda: upward(sent_off, low, k))
                env_copy(low, k, 0, sister).wait_send()

        @pl.when(high < sectors)
        def _():
            for k in range(CHUNKS):
                pl.when(even)(lambda: downward(sent_off, high, k))
                env_copy(high, k, 0, sister).wait_send()

        return carry

    lax.fori_loop(1, chips, drain_env, 0)

    def drain_sums(sector, carry):
        pl.when(sector // share != group)(lambda: sum_copy(sector).wait_send())
        return carry

    lax.fori_loop(0, sectors, drain_sums, 0)


def shards(psi, left_env, right_env, left_live, right_live):
    groups, sectors = lax.axis_size("ops"), lax.axis_size("blk")
    terms, size, width = left_env.shape[0], left_env.shape[2], right_env.shape[2]
    share = sectors // groups
    bf16, f32 = jnp.bfloat16, jnp.float32
    buffers = [
        ((size, sectors * width), bf16),
        ((terms, size, size), bf16),
        ((sectors, terms, size, width), bf16),
        ((sectors, terms, width, width), bf16),
        ((sectors, size, width), bf16),
        ((groups, share, size, width), bf16),
        ((share, size, width), f32),
    ]
    dma = pltpu.SemaphoreType.DMA
    return pl.pallas_call(
        functools.partial(kernel, groups, sectors),
        out_shape=pltpu.VMEM((size, share * width), f32),
        in_specs=[pl.BlockSpec(memory_space=pltpu.HBM)] * 5,
        out_specs=pl.BlockSpec(memory_space=pltpu.VMEM),
        scratch_shapes=[pltpu.SMEM((sectors,), jnp.int32)] * 2 + [pltpu.VMEM(shape, kind) for shape, kind in buffers] + [
            dma((5,)),
            dma((sectors, 5, CHUNKS)),
            dma((sectors, CHUNKS)),
            dma((sectors,)),
            dma((groups, share)),
        ],
        compiler_params=pltpu.CompilerParams(
            collective_id=0, has_side_effects=True,
            vmem_limit_bytes=VMEM,
        ),
    )(left_live, right_live, psi, left_env, right_env)


def solution(mesh):
    in_specs = (P("blk", None), P("ops", "blk", None, None), P("ops", "blk", None, None), P(), P())
    out_specs = P("blk", "ops")
    return jax.shard_map(shards, mesh=mesh, in_specs=in_specs, out_specs=out_specs, check_vma=False)
```

```python
import functools

import jax
import jax.numpy as jnp
from jax import lax
from jax.experimental import pallas as pl
from jax.experimental.pallas import tpu as pltpu
from jax.sharding import PartitionSpec as P

MESH = pl.DeviceIdType.MESH
CHUNKS = 2
VMEM = 60 << 20


def kernel(
    groups, sectors, left_hbm, right_hbm, psi, left, right, out,
    left_live, right_live, psi_v, left_v, mixed, rights, sent, landed, own,
    local_sem, env_send, env_recv, sum_send, sum_recv,
):
    terms, size, width = left.shape[0], left.shape[2], right.shape[2]
    share = sectors // groups
    chips = sectors // 2
    part = terms // CHUNKS
    group, me = lax.axis_index("ops"), lax.axis_index("blk")
    chip, core = me // 2, me % 2
    sister = 2 * chip + 1 - core
    has_prev, has_next = chip > 0, chip < chips - 1

    load_psi = pltpu.make_async_copy(psi, psi_v, local_sem.at[0])
    load_left = pltpu.make_async_copy(left.at[:, 0], left_v, local_sem.at[1])
    load_right = pltpu.make_async_copy(right.at[:, 0], rights.at[me], local_sem.at[2])
    load_left_live = pltpu.make_async_copy(left_hbm, left_live, local_sem.at[3])
    load_right_live = pltpu.make_async_copy(right_hbm, right_live, local_sem.at[4])
    load_left_live.start()
    load_right_live.start()
    load_psi.start()
    load_left.start()
    load_right.start()

    barrier = pltpu.get_barrier_semaphore()

    def greet(where):
        pl.semaphore_signal(barrier, inc=1, device_id=where, device_id_type=MESH)

    greet({"blk": sister})
    pl.when(has_prev)(lambda: greet({"blk": me - 2}))
    pl.when(has_next)(lambda: greet({"blk": me + 2}))
    for step in range(1, groups):
        greet({"ops": (group + step) % groups})
    pl.semaphore_wait(barrier, groups + has_prev.astype(jnp.int32) + has_next.astype(jnp.int32))

    def pieces(k):
        return pl.ds(k * part, part)

    def env_copy(sector, k, way, target, source=None):
        landing = rights.at[sector, pieces(k)]
        return pltpu.make_async_remote_copy(
            src_ref=landing if source is None else source,
            dst_ref=landing,
            send_sem=env_send.at[sector, way, k],
            recv_sem=env_recv.at[sector, k],
            device_id={"blk": target},
            device_id_type=MESH,
        )

    def own_copy(k, way, target):
        return env_copy(me, k, way, target, right.at[pieces(k), 0])

    last = CHUNKS - 1
    span = max(share // 2, 1)

    def held_group(end, side):
        return jnp.where(group == end // span, jnp.where(side == 0, 1, groups - 2), group)

    def held(end, side, at):
        return (at // span == held_group(end, side)) & (at != end)

    def each_held(end, side, use):
        for n in range(span):
            at = held_group(end, side) * span + n
            pl.when(at != end)(functools.partial(use, 2 * at + side))

    first_end, last_end = 0, chips - 1
    at_first, at_last = chip == first_end, chip == last_end

    def up_now(at, k):
        if k < last:
            return has_next
        return has_next & jnp.logical_not((chip == last_end - 1) & held(last_end, core, at))

    def down_now(at, k):
        if k < last:
            return has_prev
        return has_prev & jnp.logical_not((chip == first_end + 1) & held(first_end, core, at))

    for k in range(CHUNKS):
        pl.when(up_now(chip, k))(lambda: own_copy(k, 1, me + 2).start())
        pl.when(down_now(chip, k))(lambda: own_copy(k, 2, me - 2).start())
        own_copy(k, 0, sister).start()

    row = lax.broadcasted_iota(jnp.int32, (size, width), 0)
    lane = lax.broadcasted_iota(jnp.int32, (size, width), 1)
    load_left_live.wait()
    load_right_live.wait()
    row_live = row < left_live[me]

    load_psi.wait()
    load_left.wait()
    stacked = left_v[...].reshape(terms * size, size)

    def mix(pair, carry):
        blocks = []
        for half in range(2):
            sector = 2 * pair + half
            block = psi_v[:, pl.ds(pl.multiple_of(sector * width, width), width)].astype(jnp.float32)
            live = row_live & (lane < right_live[sector])
            blocks.append(jnp.where(live, block, 0.0).astype(jnp.bfloat16))
        both = jnp.dot(stacked, jnp.concatenate(blocks, axis=1), preferred_element_type=jnp.float32)
        both = both.astype(jnp.bfloat16)
        for half in range(2):
            mixed[2 * pair + half] = both[:, half * width:(half + 1) * width].reshape(terms, size, width)
        return carry

    lax.fori_loop(0, chips, mix, 0)

    def sum_copy(sector):
        return pltpu.make_async_remote_copy(
            src_ref=sent.at[sector],
            dst_ref=landed.at[group, sector % share],
            send_sem=sum_send.at[sector],
            recv_sem=sum_recv.at[group, sector % share],
            device_id={"ops": sector // share},
            device_id_type=MESH,
        )

    def finish(sector):
        lhs = jnp.concatenate([mixed[sector, w] for w in range(terms)], axis=1)
        rhs = jnp.concatenate([rights[sector, w] for w in range(terms)], axis=1)
        value = lax.dot_general(lhs, rhs, (((1,), (1,)), ((), ())), preferred_element_type=jnp.float32)
        mine = sector // share == group

        @pl.when(mine)
        def _():
            own[sector % share] = value

        @pl.when(jnp.logical_not(mine))
        def _():
            sent[sector] = value.astype(sent.dtype)
            sum_copy(sector).start()

    def arrive(sector):
        for k in range(CHUNKS):
            env_copy(sector, k, 0, sister).wait_recv()

    def late_below(side, at):
        return at_last & held(last_end, side, at)

    def late_above(side, at):
        return at_first & held(first_end, side, at)

    def relay(distance, k):
        low, high = me - 2 * distance, me + 2 * distance
        below, above = low >= 0, high < sectors
        if k == last:
            below = below & jnp.logical_not(late_below(core, chip - distance))
            above = above & jnp.logical_not(late_above(core, chip + distance))

        @pl.when(below)
        def _():
            env_copy(low, k, 0, sister).wait_recv()
            pl.when(up_now(chip - distance, k))(lambda: env_copy(low, k, 1, me + 2).start())
            env_copy(low, k, 0, sister).start()

        @pl.when(above)
        def _():
            env_copy(high, k, 0, sister).wait_recv()
            pl.when(down_now(chip + distance, k))(lambda: env_copy(high, k, 2, me - 2).start())
            env_copy(high, k, 0, sister).start()

    def finish_sister(sector):
        arrive(sector)
        finish(sector)

    load_right.wait()

    def step(distance, carry):
        behind = distance - 1
        low, high = me - 2 * behind, me + 2 * behind
        below, above = low >= 0, (high < sectors) & (behind > 0)

        def due(side):
            under = below & jnp.logical_not(late_below(side, chip - behind) & (behind > 0))
            return under, above & jnp.logical_not(late_above(side, chip + behind))

        under, over = due(core)
        relay(distance, 0)
        pl.when(under)(lambda: finish(low))
        pl.when(over)(lambda: finish(high))
        for k in range(1, CHUNKS):
            relay(distance, k)

        @pl.when(distance == max(chips - 2, 1))
        def _():
            pl.when(chip == first_end + 1)(lambda: each_held(
                first_end, core, lambda sector: env_copy(sector, last, 2, me - 2).start()))
            pl.when(chip == last_end - 1)(lambda: each_held(
                last_end, core, lambda sector: env_copy(sector, last, 1, me + 2).start()))

        under, over = due(1 - core)
        pl.when(under)(lambda: finish_sister(sister - 2 * behind))
        pl.when(over)(lambda: finish_sister(sister + 2 * behind))
        return carry

    lax.fori_loop(1, chips + 1, step, 0)

    def take(sector):
        env_copy(sector, last, 0, sister).wait_recv()
        env_copy(sector, last, 0, sister).start()

    @pl.when(at_first | at_last)
    def _():
        end = jnp.where(at_first, first_end, last_end)
        each_held(end, core, take)
        each_held(end, core, finish)
        each_held(end, 1 - core, finish_sister)

    def gather(slot, carry):
        total = own[slot]
        for turn in range(1, groups):
            source = (group + turn) % groups
            pltpu.make_async_remote_copy(
                src_ref=sent.at[slot],
                dst_ref=landed.at[source, slot],
                send_sem=sum_send.at[slot],
                recv_sem=sum_recv.at[source, slot],
                device_id={"ops": source},
                device_id_type=MESH,
            ).wait_recv()
            total = total + landed[source, slot].astype(jnp.float32)
        live = row_live & (lane < right_live[group * share + slot])
        out[:, pl.ds(pl.multiple_of(slot * width, width), width)] = jnp.where(live, total, 0.0)
        return carry

    lax.fori_loop(0, share, gather, 0)

    for k in range(CHUNKS):
        pl.when(has_next)(lambda: own_copy(k, 1, me + 2).wait_send())
        pl.when(has_prev)(lambda: own_copy(k, 2, me - 2).wait_send())
        own_copy(k, 0, sister).wait_send()

    def drain_env(distance, carry):
        low, high = me - 2 * distance, me + 2 * distance

        @pl.when(low >= 0)
        def _():
            for k in range(CHUNKS):
                pl.when(has_next)(lambda: env_copy(low, k, 1, me + 2).wait_send())
                env_copy(low, k, 0, sister).wait_send()

        @pl.when(high < sectors)
        def _():
            for k in range(CHUNKS):
                pl.when(has_prev)(lambda: env_copy(high, k, 2, me - 2).wait_send())
                env_copy(high, k, 0, sister).wait_send()

        return carry

    lax.fori_loop(1, chips, drain_env, 0)

    def drain_sums(sector, carry):
        pl.when(sector // share != group)(lambda: sum_copy(sector).wait_send())
        return carry

    lax.fori_loop(0, sectors, drain_sums, 0)


def shards(psi, left_env, right_env, left_live, right_live):
    groups, sectors = lax.axis_size("ops"), lax.axis_size("blk")
    terms, size, width = left_env.shape[0], left_env.shape[2], right_env.shape[2]
    share = sectors // groups
    bf16, f32 = jnp.bfloat16, jnp.float32
    buffers = [
        ((size, sectors * width), bf16),
        ((terms, size, size), bf16),
        ((sectors, terms, size, width), bf16),
        ((sectors, terms, width, width), bf16),
        ((sectors, size, width), bf16),
        ((groups, share, size, width), bf16),
        ((share, size, width), f32),
    ]
    dma = pltpu.SemaphoreType.DMA
    return pl.pallas_call(
        functools.partial(kernel, groups, sectors),
        out_shape=pltpu.VMEM((size, share * width), f32),
        in_specs=[pl.BlockSpec(memory_space=pltpu.HBM)] * 5,
        out_specs=pl.BlockSpec(memory_space=pltpu.VMEM),
        scratch_shapes=[pltpu.SMEM((sectors,), jnp.int32)] * 2 + [pltpu.VMEM(shape, kind) for shape, kind in buffers] + [
            dma((5,)),
            dma((sectors, 3, CHUNKS)),
            dma((sectors, CHUNKS)),
            dma((sectors,)),
            dma((groups, share)),
        ],
        compiler_params=pltpu.CompilerParams(
            collective_id=0, has_side_effects=True,
            vmem_limit_bytes=VMEM,
        ),
    )(left_live, right_live, psi, left_env, right_env)


def solution(mesh):
    in_specs = (P("blk", None), P("ops", "blk", None, None), P("ops", "blk", None, None), P(), P())
    out_specs = P("blk", "ops")
    return jax.shard_map(shards, mesh=mesh, in_specs=in_specs, out_specs=out_specs, check_vma=False)
```

```python
import functools

import jax
import jax.numpy as jnp
from jax import lax
from jax.experimental import pallas as pl
from jax.experimental.pallas import tpu as pltpu
from jax.sharding import PartitionSpec as P

MESH = pl.DeviceIdType.MESH
CHUNKS = 4
VMEM = 60 << 20


def kernel(
    groups, sectors, left_hbm, right_hbm, psi, left, right, out,
    left_live, right_live, psi_v, left_v, mixed, rights, sent, landed, own,
    local_sem, env_send, env_recv, sum_send, sum_recv,
):
    terms, size, width = left.shape[0], left.shape[2], right.shape[2]
    share = sectors // groups
    chips = sectors // 2
    part = terms // CHUNKS
    group, me = lax.axis_index("ops"), lax.axis_index("blk")
    chip, core = me // 2, me % 2
    sister = 2 * chip + 1 - core
    has_prev, has_next = chip > 0, chip < chips - 1

    load_psi = pltpu.make_async_copy(psi, psi_v, local_sem.at[0])
    load_left = pltpu.make_async_copy(left.at[:, 0], left_v, local_sem.at[1])
    load_right = pltpu.make_async_copy(right.at[:, 0], rights.at[me], local_sem.at[2])
    load_left_live = pltpu.make_async_copy(left_hbm, left_live, local_sem.at[3])
    load_right_live = pltpu.make_async_copy(right_hbm, right_live, local_sem.at[4])
    load_left_live.start()
    load_right_live.start()
    load_psi.start()
    load_left.start()
    load_right.start()

    barrier = pltpu.get_barrier_semaphore()

    def greet(where):
        pl.semaphore_signal(barrier, inc=1, device_id=where, device_id_type=MESH)

    greet({"blk": sister})
    pl.when(has_prev)(lambda: greet({"blk": me - 2}))
    pl.when(has_next)(lambda: greet({"blk": me + 2}))
    for step in range(1, groups):
        greet({"ops": (group + step) % groups})
    pl.semaphore_wait(barrier, groups + has_prev.astype(jnp.int32) + has_next.astype(jnp.int32))

    def pieces(k):
        return pl.ds(k * part, part)

    def env_copy(sector, k, way, target, source=None):
        landing = rights.at[sector, pieces(k)]
        return pltpu.make_async_remote_copy(
            src_ref=landing if source is None else source,
            dst_ref=landing,
            send_sem=env_send.at[sector, way, k],
            recv_sem=env_recv.at[sector, k],
            device_id={"blk": target},
            device_id_type=MESH,
        )

    def own_copy(k, way, target):
        return env_copy(me, k, way, target, right.at[pieces(k), 0])

    last = CHUNKS - 1
    span = max(share // 2, 1)

    def held_group(end, side):
        return jnp.where(group == end // span, jnp.where(side == 0, 1, groups - 2), group)

    def held(end, side, at):
        return (at // span == held_group(end, side)) & (at != end)

    def each_held(end, side, use):
        for n in range(span):
            at = held_group(end, side) * span + n
            pl.when(at != end)(functools.partial(use, 2 * at + side))

    first_end, last_end = 0, chips - 1
    at_first, at_last = chip == first_end, chip == last_end

    def up_now(at, k):
        if k < last:
            return has_next
        return has_next & jnp.logical_not((chip == last_end - 1) & held(last_end, core, at))

    def down_now(at, k):
        if k < last:
            return has_prev
        return has_prev & jnp.logical_not((chip == first_end + 1) & held(first_end, core, at))

    for k in range(CHUNKS):
        pl.when(up_now(chip, k))(lambda: own_copy(k, 1, me + 2).start())
        pl.when(down_now(chip, k))(lambda: own_copy(k, 2, me - 2).start())
        own_copy(k, 0, sister).start()

    row = lax.broadcasted_iota(jnp.int32, (size, width), 0)
    lane = lax.broadcasted_iota(jnp.int32, (size, width), 1)
    load_left_live.wait()
    load_right_live.wait()
    row_live = row < left_live[me]

    load_psi.wait()
    load_left.wait()
    stacked = left_v[...].reshape(terms * size, size)

    def mix(pair, carry):
        blocks = []
        for half in range(2):
            sector = 2 * pair + half
            block = psi_v[:, pl.ds(pl.multiple_of(sector * width, width), width)].astype(jnp.float32)
            live = row_live & (lane < right_live[sector])
            blocks.append(jnp.where(live, block, 0.0).astype(jnp.bfloat16))
        both = jnp.dot(stacked, jnp.concatenate(blocks, axis=1), preferred_element_type=jnp.float32)
        both = both.astype(jnp.bfloat16)
        for half in range(2):
            mixed[2 * pair + half] = both[:, half * width:(half + 1) * width].reshape(terms, size, width)
        return carry

    lax.fori_loop(0, chips, mix, 0)

    def sum_copy(sector):
        return pltpu.make_async_remote_copy(
            src_ref=sent.at[sector],
            dst_ref=landed.at[group, sector % share],
            send_sem=sum_send.at[sector],
            recv_sem=sum_recv.at[group, sector % share],
            device_id={"ops": sector // share},
            device_id_type=MESH,
        )

    def finish(sector):
        lhs = jnp.concatenate([mixed[sector, w] for w in range(terms)], axis=1)
        rhs = jnp.concatenate([rights[sector, w] for w in range(terms)], axis=1)
        value = lax.dot_general(lhs, rhs, (((1,), (1,)), ((), ())), preferred_element_type=jnp.float32)
        mine = sector // share == group

        @pl.when(mine)
        def _():
            own[sector % share] = value

        @pl.when(jnp.logical_not(mine))
        def _():
            sent[sector] = value.astype(sent.dtype)
            sum_copy(sector).start()

    def arrive(sector):
        for k in range(CHUNKS):
            env_copy(sector, k, 0, sister).wait_recv()

    def late_below(side, at):
        return at_last & held(last_end, side, at)

    def late_above(side, at):
        return at_first & held(first_end, side, at)

    def relay(distance, k):
        low, high = me - 2 * distance, me + 2 * distance
        below, above = low >= 0, high < sectors
        if k == last:
            below = below & jnp.logical_not(late_below(core, chip - distance))
            above = above & jnp.logical_not(late_above(core, chip + distance))

        @pl.when(below)
        def _():
            env_copy(low, k, 0, sister).wait_recv()
            pl.when(up_now(chip - distance, k))(lambda: env_copy(low, k, 1, me + 2).start())
            env_copy(low, k, 0, sister).start()

        @pl.when(above)
        def _():
            env_copy(high, k, 0, sister).wait_recv()
            pl.when(down_now(chip + distance, k))(lambda: env_copy(high, k, 2, me - 2).start())
            env_copy(high, k, 0, sister).start()

    def finish_sister(sector):
        arrive(sector)
        finish(sector)

    load_right.wait()

    def step(distance, carry):
        behind = distance - 1
        low, high = me - 2 * behind, me + 2 * behind
        below, above = low >= 0, (high < sectors) & (behind > 0)

        def due(side):
            under = below & jnp.logical_not(late_below(side, chip - behind) & (behind > 0))
            return under, above & jnp.logical_not(late_above(side, chip + behind))

        under, over = due(core)
        relay(distance, 0)
        pl.when(under)(lambda: finish(low))
        pl.when(over)(lambda: finish(high))
        for k in range(1, CHUNKS):
            relay(distance, k)

        @pl.when(distance == max(chips - 2, 1))
        def _():
            pl.when(chip == first_end + 1)(lambda: each_held(
                first_end, core, lambda sector: env_copy(sector, last, 2, me - 2).start()))
            pl.when(chip == last_end - 1)(lambda: each_held(
                last_end, core, lambda sector: env_copy(sector, last, 1, me + 2).start()))

        under, over = due(1 - core)
        pl.when(under)(lambda: finish_sister(sister - 2 * behind))
        pl.when(over)(lambda: finish_sister(sister + 2 * behind))
        return carry

    lax.fori_loop(1, chips + 1, step, 0)

    def take(sector):
        env_copy(sector, last, 0, sister).wait_recv()
        env_copy(sector, last, 0, sister).start()

    @pl.when(at_first | at_last)
    def _():
        end = jnp.where(at_first, first_end, last_end)
        each_held(end, core, take)
        each_held(end, core, finish)
        each_held(end, 1 - core, finish_sister)

    def gather(slot, carry):
        total = own[slot]
        for turn in range(1, groups):
            source = (group + turn) % groups
            pltpu.make_async_remote_copy(
                src_ref=sent.at[slot],
                dst_ref=landed.at[source, slot],
                send_sem=sum_send.at[slot],
                recv_sem=sum_recv.at[source, slot],
                device_id={"ops": source},
                device_id_type=MESH,
            ).wait_recv()
            total = total + landed[source, slot].astype(jnp.float32)
        live = row_live & (lane < right_live[group * share + slot])
        out[:, pl.ds(pl.multiple_of(slot * width, width), width)] = jnp.where(live, total, 0.0)
        return carry

    lax.fori_loop(0, share, gather, 0)

    for k in range(CHUNKS):
        pl.when(has_next)(lambda: own_copy(k, 1, me + 2).wait_send())
        pl.when(has_prev)(lambda: own_copy(k, 2, me - 2).wait_send())
        own_copy(k, 0, sister).wait_send()

    def drain_env(distance, carry):
        low, high = me - 2 * distance, me + 2 * distance

        @pl.when(low >= 0)
        def _():
            for k in range(CHUNKS):
                pl.when(has_next)(lambda: env_copy(low, k, 1, me + 2).wait_send())
                env_copy(low, k, 0, sister).wait_send()

        @pl.when(high < sectors)
        def _():
            for k in range(CHUNKS):
                pl.when(has_prev)(lambda: env_copy(high, k, 2, me - 2).wait_send())
                env_copy(high, k, 0, sister).wait_send()

        return carry

    lax.fori_loop(1, chips, drain_env, 0)

    def drain_sums(sector, carry):
        pl.when(sector // share != group)(lambda: sum_copy(sector).wait_send())
        return carry

    lax.fori_loop(0, sectors, drain_sums, 0)


def shards(psi, left_env, right_env, left_live, right_live):
    groups, sectors = lax.axis_size("ops"), lax.axis_size("blk")
    terms, size, width = left_env.shape[0], left_env.shape[2], right_env.shape[2]
    share = sectors // groups
    bf16, f32 = jnp.bfloat16, jnp.float32
    buffers = [
        ((size, sectors * width), bf16),
        ((terms, size, size), bf16),
        ((sectors, terms, size, width), bf16),
        ((sectors, terms, width, width), bf16),
        ((sectors, size, width), bf16),
        ((groups, share, size, width), bf16),
        ((share, size, width), f32),
    ]
    dma = pltpu.SemaphoreType.DMA
    return pl.pallas_call(
        functools.partial(kernel, groups, sectors),
        out_shape=pltpu.VMEM((size, share * width), f32),
        in_specs=[pl.BlockSpec(memory_space=pltpu.HBM)] * 5,
        out_specs=pl.BlockSpec(memory_space=pltpu.VMEM),
        scratch_shapes=[pltpu.SMEM((sectors,), jnp.int32)] * 2 + [pltpu.VMEM(shape, kind) for shape, kind in buffers] + [
            dma((5,)),
            dma((sectors, 3, CHUNKS)),
            dma((sectors, CHUNKS)),
            dma((sectors,)),
            dma((groups, share)),
        ],
        compiler_params=pltpu.CompilerParams(
            collective_id=0, has_side_effects=True,
            vmem_limit_bytes=VMEM,
        ),
    )(left_live, right_live, psi, left_env, right_env)


def solution(mesh):
    in_specs = (P("blk", None), P("ops", "blk", None, None), P("ops", "blk", None, None), P(), P())
    out_specs = P("blk", "ops")
    return jax.shard_map(shards, mesh=mesh, in_specs=in_specs, out_specs=out_specs, check_vma=False)
```

```python
import functools

import jax
import jax.numpy as jnp
from jax import lax
from jax.experimental import pallas as pl
from jax.experimental.pallas import tpu as pltpu
from jax.sharding import PartitionSpec as P

MESH = pl.DeviceIdType.MESH
CHUNKS = 4
VMEM = 60 << 20


def kernel(
    groups, sectors, left_hbm, right_hbm, psi, left, right, out,
    left_live, right_live, psi_v, left_v, mixed, rights, sent, landed, own,
    local_sem, env_send, env_recv, sum_send, sum_recv,
):
    terms, size, width = left.shape[0], left.shape[2], right.shape[2]
    share = sectors // groups
    chips = sectors // 2
    part = terms // CHUNKS
    group, me = lax.axis_index("ops"), lax.axis_index("blk")
    chip, core = me // 2, me % 2
    sister = 2 * chip + 1 - core
    has_prev, has_next = chip > 0, chip < chips - 1

    load_psi = pltpu.make_async_copy(psi, psi_v, local_sem.at[0])
    load_left = pltpu.make_async_copy(left.at[:, 0], left_v, local_sem.at[1])
    load_right = pltpu.make_async_copy(right.at[:, 0], rights.at[me], local_sem.at[2])
    load_left_live = pltpu.make_async_copy(left_hbm, left_live, local_sem.at[3])
    load_right_live = pltpu.make_async_copy(right_hbm, right_live, local_sem.at[4])
    load_left_live.start()
    load_right_live.start()
    load_psi.start()
    load_left.start()
    load_right.start()

    barrier = pltpu.get_barrier_semaphore()

    def greet(where):
        pl.semaphore_signal(barrier, inc=1, device_id=where, device_id_type=MESH)

    greet({"blk": sister})
    pl.when(has_prev)(lambda: greet({"blk": me - 2}))
    pl.when(has_next)(lambda: greet({"blk": me + 2}))
    for step in range(1, groups):
        greet({"ops": (group + step) % groups})
    pl.semaphore_wait(barrier, groups + has_prev.astype(jnp.int32) + has_next.astype(jnp.int32))

    def pieces(k):
        return pl.ds(k * part, part)

    def env_copy(sector, k, way, target, source=None):
        landing = rights.at[sector, pieces(k)]
        return pltpu.make_async_remote_copy(
            src_ref=landing if source is None else source,
            dst_ref=landing,
            send_sem=env_send.at[sector, way, k],
            recv_sem=env_recv.at[sector, k],
            device_id={"blk": target},
            device_id_type=MESH,
        )

    def own_copy(k, way, target):
        return env_copy(me, k, way, target, right.at[pieces(k), 0])

    late = range(1, CHUNKS)
    span = max(share // 2, 1)

    def held_group(end, side):
        return jnp.where(group == end // span, jnp.where(side == 0, 1, groups - 2), group)

    def held(end, side, at):
        return (at // span == held_group(end, side)) & (at != end)

    def each_held(end, side, use):
        for n in range(span):
            at = held_group(end, side) * span + n
            pl.when(at != end)(functools.partial(use, 2 * at + side))

    first_end, last_end = 0, chips - 1
    at_first, at_last = chip == first_end, chip == last_end

    def up_now(at, k):
        if k not in late:
            return has_next
        return has_next & jnp.logical_not((chip == last_end - 1) & held(last_end, core, at))

    def down_now(at, k):
        if k not in late:
            return has_prev
        return has_prev & jnp.logical_not((chip == first_end + 1) & held(first_end, core, at))

    for k in range(CHUNKS):
        pl.when(up_now(chip, k))(lambda: own_copy(k, 1, me + 2).start())
        pl.when(down_now(chip, k))(lambda: own_copy(k, 2, me - 2).start())
        own_copy(k, 0, sister).start()

    row = lax.broadcasted_iota(jnp.int32, (size, width), 0)
    lane = lax.broadcasted_iota(jnp.int32, (size, width), 1)
    load_left_live.wait()
    load_right_live.wait()
    row_live = row < left_live[me]

    load_psi.wait()
    load_left.wait()
    stacked = left_v[...].reshape(terms * size, size)

    def mix(pair, carry):
        blocks = []
        for half in range(2):
            sector = 2 * pair + half
            block = psi_v[:, pl.ds(pl.multiple_of(sector * width, width), width)].astype(jnp.float32)
            live = row_live & (lane < right_live[sector])
            blocks.append(jnp.where(live, block, 0.0).astype(jnp.bfloat16))
        both = jnp.dot(stacked, jnp.concatenate(blocks, axis=1), preferred_element_type=jnp.float32)
        both = both.astype(jnp.bfloat16)
        for half in range(2):
            mixed[2 * pair + half] = both[:, half * width:(half + 1) * width].reshape(terms, size, width)
        return carry

    def late_below(side, at):
        return at_last & held(last_end, side, at)

    def late_above(side, at):
        return at_first & held(first_end, side, at)

    def relay(distance, k):
        low, high = me - 2 * distance, me + 2 * distance
        below, above = low >= 0, high < sectors
        if k in late:
            below = below & jnp.logical_not(late_below(core, chip - distance))
            above = above & jnp.logical_not(late_above(core, chip + distance))

        @pl.when(below)
        def _():
            env_copy(low, k, 0, sister).wait_recv()
            pl.when(up_now(chip - distance, k))(lambda: env_copy(low, k, 1, me + 2).start())
            env_copy(low, k, 0, sister).start()

        @pl.when(above)
        def _():
            env_copy(high, k, 0, sister).wait_recv()
            pl.when(down_now(chip + distance, k))(lambda: env_copy(high, k, 2, me - 2).start())
            env_copy(high, k, 0, sister).start()

    lax.fori_loop(0, chips // 2, mix, 0)
    relay(1, 0)
    lax.fori_loop(chips // 2, chips, mix, 0)

    def sum_copy(sector):
        return pltpu.make_async_remote_copy(
            src_ref=sent.at[sector],
            dst_ref=landed.at[group, sector % share],
            send_sem=sum_send.at[sector],
            recv_sem=sum_recv.at[group, sector % share],
            device_id={"ops": sector // share},
            device_id_type=MESH,
        )

    def finish(sector):
        lhs = jnp.concatenate([mixed[sector, w] for w in range(terms)], axis=1)
        rhs = jnp.concatenate([rights[sector, w] for w in range(terms)], axis=1)
        value = lax.dot_general(lhs, rhs, (((1,), (1,)), ((), ())), preferred_element_type=jnp.float32)
        mine = sector // share == group

        @pl.when(mine)
        def _():
            own[sector % share] = value

        @pl.when(jnp.logical_not(mine))
        def _():
            sent[sector] = value.astype(sent.dtype)
            sum_copy(sector).start()

    def arrive(sector):
        for k in range(CHUNKS):
            env_copy(sector, k, 0, sister).wait_recv()

    def finish_sister(sector):
        arrive(sector)
        finish(sector)

    load_right.wait()

    def step(distance, carry):
        behind = distance - 1
        low, high = me - 2 * behind, me + 2 * behind
        below, above = low >= 0, (high < sectors) & (behind > 0)

        def due(side):
            under = below & jnp.logical_not(late_below(side, chip - behind) & (behind > 0))
            return under, above & jnp.logical_not(late_above(side, chip + behind))

        under, over = due(core)
        pl.when(distance > 1)(lambda: relay(distance, 0))
        pl.when(under)(lambda: finish(low))
        pl.when(over)(lambda: finish(high))
        for k in range(1, CHUNKS):
            relay(distance, k)

        @pl.when(distance == max(chips - 2, 1))
        def _():
            def release(way, target, sector):
                for k in late:
                    env_copy(sector, k, way, target).start()

            pl.when(chip == first_end + 1)(lambda: each_held(
                first_end, core, functools.partial(release, 2, me - 2)))
            pl.when(chip == last_end - 1)(lambda: each_held(
                last_end, core, functools.partial(release, 1, me + 2)))

        under, over = due(1 - core)
        pl.when(under)(lambda: finish_sister(sister - 2 * behind))
        pl.when(over)(lambda: finish_sister(sister + 2 * behind))
        return carry

    lax.fori_loop(1, chips + 1, step, 0)

    def take(sector):
        for k in late:
            env_copy(sector, k, 0, sister).wait_recv()
            env_copy(sector, k, 0, sister).start()

    @pl.when(at_first | at_last)
    def _():
        end = jnp.where(at_first, first_end, last_end)
        each_held(end, core, take)
        each_held(end, core, finish)
        each_held(end, 1 - core, finish_sister)

    def gather(slot, carry):
        total = own[slot]
        for turn in range(1, groups):
            source = (group + turn) % groups
            pltpu.make_async_remote_copy(
                src_ref=sent.at[slot],
                dst_ref=landed.at[source, slot],
                send_sem=sum_send.at[slot],
                recv_sem=sum_recv.at[source, slot],
                device_id={"ops": source},
                device_id_type=MESH,
            ).wait_recv()
            total = total + landed[source, slot].astype(jnp.float32)
        live = row_live & (lane < right_live[group * share + slot])
        out[:, pl.ds(pl.multiple_of(slot * width, width), width)] = jnp.where(live, total, 0.0)
        return carry

    lax.fori_loop(0, share, gather, 0)

    for k in range(CHUNKS):
        pl.when(has_next)(lambda: own_copy(k, 1, me + 2).wait_send())
        pl.when(has_prev)(lambda: own_copy(k, 2, me - 2).wait_send())
        own_copy(k, 0, sister).wait_send()

    def drain_env(distance, carry):
        low, high = me - 2 * distance, me + 2 * distance

        @pl.when(low >= 0)
        def _():
            for k in range(CHUNKS):
                pl.when(has_next)(lambda: env_copy(low, k, 1, me + 2).wait_send())
                env_copy(low, k, 0, sister).wait_send()

        @pl.when(high < sectors)
        def _():
            for k in range(CHUNKS):
                pl.when(has_prev)(lambda: env_copy(high, k, 2, me - 2).wait_send())
                env_copy(high, k, 0, sister).wait_send()

        return carry

    lax.fori_loop(1, chips, drain_env, 0)

    def drain_sums(sector, carry):
        pl.when(sector // share != group)(lambda: sum_copy(sector).wait_send())
        return carry

    lax.fori_loop(0, sectors, drain_sums, 0)


def shards(psi, left_env, right_env, left_live, right_live):
    groups, sectors = lax.axis_size("ops"), lax.axis_size("blk")
    terms, size, width = left_env.shape[0], left_env.shape[2], right_env.shape[2]
    share = sectors // groups
    bf16, f32 = jnp.bfloat16, jnp.float32
    buffers = [
        ((size, sectors * width), bf16),
        ((terms, size, size), bf16),
        ((sectors, terms, size, width), bf16),
        ((sectors, terms, width, width), bf16),
        ((sectors, size, width), bf16),
        ((groups, share, size, width), bf16),
        ((share, size, width), f32),
    ]
    dma = pltpu.SemaphoreType.DMA
    return pl.pallas_call(
        functools.partial(kernel, groups, sectors),
        out_shape=pltpu.VMEM((size, share * width), f32),
        in_specs=[pl.BlockSpec(memory_space=pltpu.HBM)] * 5,
        out_specs=pl.BlockSpec(memory_space=pltpu.VMEM),
        scratch_shapes=[pltpu.SMEM((sectors,), jnp.int32)] * 2 + [pltpu.VMEM(shape, kind) for shape, kind in buffers] + [
            dma((5,)),
            dma((sectors, 3, CHUNKS)),
            dma((sectors, CHUNKS)),
            dma((sectors,)),
            dma((groups, share)),
        ],
        compiler_params=pltpu.CompilerParams(
            collective_id=0, has_side_effects=True,
            vmem_limit_bytes=VMEM,
        ),
    )(left_live, right_live, psi, left_env, right_env)


def solution(mesh):
    in_specs = (P("blk", None), P("ops", "blk", None, None), P("ops", "blk", None, None), P(), P())
    out_specs = P("blk", "ops")
    return jax.shard_map(shards, mesh=mesh, in_specs=in_specs, out_specs=out_specs, check_vma=False)
```

```python
import functools

import jax
import jax.numpy as jnp
from jax import lax
from jax.experimental import pallas as pl
from jax.experimental.pallas import tpu as pltpu
from jax.sharding import PartitionSpec as P

MESH = pl.DeviceIdType.MESH
CHUNKS = 4
VMEM = 60 << 20


def kernel(
    groups, sectors, left_hbm, right_hbm, psi, left, right, out,
    left_live, right_live, psi_v, left_v, mixed, rights, sent, landed, own,
    local_sem, env_send, env_recv, sum_send, sum_recv,
):
    terms, size, width = left.shape[0], left.shape[2], right.shape[2]
    share = sectors // groups
    chips = sectors // 2
    part = terms // CHUNKS
    group, me = lax.axis_index("ops"), lax.axis_index("blk")
    chip, core = me // 2, me % 2
    sister = 2 * chip + 1 - core
    following, previous = (me + 2) % sectors, (me + sectors - 2) % sectors

    load_psi = pltpu.make_async_copy(psi, psi_v, local_sem.at[0])
    load_left = pltpu.make_async_copy(left.at[:, 0], left_v, local_sem.at[1])
    load_right = pltpu.make_async_copy(right.at[:, 0], rights.at[me], local_sem.at[2])
    load_left_live = pltpu.make_async_copy(left_hbm, left_live, local_sem.at[3])
    load_right_live = pltpu.make_async_copy(right_hbm, right_live, local_sem.at[4])
    load_left_live.start()
    load_right_live.start()
    load_psi.start()
    load_left.start()
    load_right.start()

    barrier = pltpu.get_barrier_semaphore()

    def greet(where):
        pl.semaphore_signal(barrier, inc=1, device_id=where, device_id_type=MESH)

    greet({"blk": sister})
    greet({"blk": previous})
    greet({"blk": following})
    for step in range(1, groups):
        greet({"ops": (group + step) % groups})
    pl.semaphore_wait(barrier, groups + 2)

    def pieces(k):
        return pl.ds(k * part, part)

    def env_copy(sector, k, way, target, source=None):
        landing = rights.at[sector, pieces(k)]
        return pltpu.make_async_remote_copy(
            src_ref=landing if source is None else source,
            dst_ref=landing,
            send_sem=env_send.at[sector, way, k],
            recv_sem=env_recv.at[sector, k],
            device_id={"blk": target},
            device_id_type=MESH,
        )

    reach = (chips - 1) // 2
    halves = (range(CHUNKS // 2), range(CHUNKS // 2, CHUNKS))
    orders = (range(CHUNKS), [(k + CHUNKS // 2) % CHUNKS for k in range(CHUNKS)])

    def comes(distance, k, way):
        there = distance <= reach
        if chips % 2 == 0 and k in halves[way - 1]:
            there = there | (distance == chips // 2)
        return there

    def onward(use, sector, distance, k, way, source=None):
        target = following if way == 1 else previous
        pl.when(jnp.asarray(comes(distance + 1, k, way)))(lambda: use(env_copy(sector, k, way, target, source)))

    def start(copy):
        copy.start()

    def sent_off(copy):
        copy.wait_send()

    def own_copies(use):
        for n in range(CHUNKS):
            for way in (1, 2):
                k = orders[way - 1][n]
                onward(use, me, 0, k, way, right.at[pieces(k), 0])
            use(env_copy(me, n, 0, sister, right.at[pieces(n), 0]))

    own_copies(start)

    row = lax.broadcasted_iota(jnp.int32, (size, width), 0)
    lane = lax.broadcasted_iota(jnp.int32, (size, width), 1)
    load_left_live.wait()
    load_right_live.wait()
    row_live = row < left_live[me]

    load_psi.wait()
    load_left.wait()
    stacked = left_v[...].reshape(terms * size, size)

    def mix(pair, carry):
        blocks = []
        for half in range(2):
            sector = 2 * pair + half
            block = psi_v[:, pl.ds(pl.multiple_of(sector * width, width), width)].astype(jnp.float32)
            live = row_live & (lane < right_live[sector])
            blocks.append(jnp.where(live, block, 0.0).astype(jnp.bfloat16))
        both = jnp.dot(stacked, jnp.concatenate(blocks, axis=1), preferred_element_type=jnp.float32)
        both = both.astype(jnp.bfloat16)
        for half in range(2):
            mixed[2 * pair + half] = both[:, half * width:(half + 1) * width].reshape(terms, size, width)
        return carry

    lax.fori_loop(0, chips, mix, 0)

    def sum_copy(sector):
        return pltpu.make_async_remote_copy(
            src_ref=sent.at[sector],
            dst_ref=landed.at[group, sector % share],
            send_sem=sum_send.at[sector],
            recv_sem=sum_recv.at[group, sector % share],
            device_id={"ops": sector // share},
            device_id_type=MESH,
        )

    def finish(sector):
        lhs = jnp.concatenate([mixed[sector, w] for w in range(terms)], axis=1)
        rhs = jnp.concatenate([rights[sector, w] for w in range(terms)], axis=1)
        value = lax.dot_general(lhs, rhs, (((1,), (1,)), ((), ())), preferred_element_type=jnp.float32)
        mine = sector // share == group

        @pl.when(mine)
        def _():
            own[sector % share] = value

        @pl.when(jnp.logical_not(mine))
        def _():
            sent[sector] = value.astype(sent.dtype)
            sum_copy(sector).start()

    def arrive(sector):
        for k in range(CHUNKS):
            env_copy(sector, k, 0, sister).wait_recv()

    def at(distance, way, core_of):
        shift = 2 * distance if way == 2 else sectors - 2 * distance
        return (core_of + shift) % sectors

    def relay(distance, n):
        for way in (1, 2):
            k = orders[way - 1][n]
            sector = at(distance, way, me)

            @pl.when(comes(distance, k, way))
            def _():
                env_copy(sector, k, 0, sister).wait_recv()
                onward(start, sector, distance, k, way)
                env_copy(sector, k, 0, sister).start()

    def finish_sister(sector):
        arrive(sector)
        finish(sector)

    load_right.wait()

    def step(distance, carry):
        behind = distance - 1
        above = (behind > 0) & (2 * behind != chips)
        relay(distance, 0)
        finish(at(behind, 1, me))
        pl.when(above)(lambda: finish(at(behind, 2, me)))
        for n in range(1, CHUNKS):
            relay(distance, n)
        finish_sister(at(behind, 1, sister))
        pl.when(above)(lambda: finish_sister(at(behind, 2, sister)))
        return carry

    lax.fori_loop(1, chips // 2 + 2, step, 0)

    def gather(slot, carry):
        total = own[slot]
        for turn in range(1, groups):
            source = (group + turn) % groups
            pltpu.make_async_remote_copy(
                src_ref=sent.at[slot],
                dst_ref=landed.at[source, slot],
                send_sem=sum_send.at[slot],
                recv_sem=sum_recv.at[source, slot],
                device_id={"ops": source},
                device_id_type=MESH,
            ).wait_recv()
            total = total + landed[source, slot].astype(jnp.float32)
        live = row_live & (lane < right_live[group * share + slot])
        out[:, pl.ds(pl.multiple_of(slot * width, width), width)] = jnp.where(live, total, 0.0)
        return carry

    lax.fori_loop(0, share, gather, 0)

    own_copies(sent_off)

    def drain_env(distance, carry):
        for way in (1, 2):
            for k in range(CHUNKS):
                sector = at(distance, way, me)

                @pl.when(comes(distance, k, way))
                def _():
                    onward(sent_off, sector, distance, k, way)
                    env_copy(sector, k, 0, sister).wait_send()

        return carry

    lax.fori_loop(1, chips // 2 + 1, drain_env, 0)

    def drain_sums(sector, carry):
        pl.when(sector // share != group)(lambda: sum_copy(sector).wait_send())
        return carry

    lax.fori_loop(0, sectors, drain_sums, 0)


def shards(psi, left_env, right_env, left_live, right_live):
    groups, sectors = lax.axis_size("ops"), lax.axis_size("blk")
    terms, size, width = left_env.shape[0], left_env.shape[2], right_env.shape[2]
    share = sectors // groups
    bf16, f32 = jnp.bfloat16, jnp.float32
    buffers = [
        ((size, sectors * width), bf16),
        ((terms, size, size), bf16),
        ((sectors, terms, size, width), bf16),
        ((sectors, terms, width, width), bf16),
        ((sectors, size, width), bf16),
        ((groups, share, size, width), bf16),
        ((share, size, width), f32),
    ]
    dma = pltpu.SemaphoreType.DMA
    return pl.pallas_call(
        functools.partial(kernel, groups, sectors),
        out_shape=pltpu.VMEM((size, share * width), f32),
        in_specs=[pl.BlockSpec(memory_space=pltpu.HBM)] * 5,
        out_specs=pl.BlockSpec(memory_space=pltpu.VMEM),
        scratch_shapes=[pltpu.SMEM((sectors,), jnp.int32)] * 2 + [pltpu.VMEM(shape, kind) for shape, kind in buffers] + [
            dma((5,)),
            dma((sectors, 3, CHUNKS)),
            dma((sectors, CHUNKS)),
            dma((sectors,)),
            dma((groups, share)),
        ],
        compiler_params=pltpu.CompilerParams(
            collective_id=0, has_side_effects=True,
            vmem_limit_bytes=VMEM,
        ),
    )(left_live, right_live, psi, left_env, right_env)


def solution(mesh):
    in_specs = (P("blk", None), P("ops", "blk", None, None), P("ops", "blk", None, None), P(), P())
    out_specs = P("blk", "ops")
    return jax.shard_map(shards, mesh=mesh, in_specs=in_specs, out_specs=out_specs, check_vma=False)
```

```python
import functools

import jax
import jax.numpy as jnp
from jax import lax
from jax.experimental import pallas as pl
from jax.experimental.pallas import tpu as pltpu
from jax.sharding import PartitionSpec as P

MESH = pl.DeviceIdType.MESH
CHUNKS = 4
VMEM = 60 << 20


def kernel(
    groups, sectors, left_hbm, right_hbm, psi, left, right, out,
    left_live, right_live, psi_v, left_v, mixed, rights, sent, landed, own,
    local_sem, env_send, env_recv, sum_send, sum_recv,
):
    terms, size, width = left.shape[0], left.shape[2], right.shape[2]
    share = sectors // groups
    chips = sectors // 2
    part = terms // CHUNKS
    group, me = lax.axis_index("ops"), lax.axis_index("blk")
    chip, core = me // 2, me % 2
    sister = 2 * chip + 1 - core
    following, previous = (me + 2) % sectors, (me + sectors - 2) % sectors

    load_psi = pltpu.make_async_copy(psi, psi_v, local_sem.at[0])
    load_left = pltpu.make_async_copy(left.at[:, 0], left_v, local_sem.at[1])
    load_right = pltpu.make_async_copy(right.at[:, 0], rights.at[me], local_sem.at[2])
    load_left_live = pltpu.make_async_copy(left_hbm, left_live, local_sem.at[3])
    load_right_live = pltpu.make_async_copy(right_hbm, right_live, local_sem.at[4])
    load_left_live.start()
    load_right_live.start()
    load_psi.start()
    load_left.start()
    load_right.start()

    barrier = pltpu.get_barrier_semaphore()

    def greet(where):
        pl.semaphore_signal(barrier, inc=1, device_id=where, device_id_type=MESH)

    greet({"blk": sister})
    greet({"blk": previous})
    greet({"blk": following})
    for step in range(1, groups):
        greet({"ops": (group + step) % groups})
    pl.semaphore_wait(barrier, groups + 2)

    def pieces(k):
        return pl.ds(k * part, part)

    def env_copy(sector, k, way, target, source=None):
        landing = rights.at[sector, pieces(k)]
        return pltpu.make_async_remote_copy(
            src_ref=landing if source is None else source,
            dst_ref=landing,
            send_sem=env_send.at[sector, way, k],
            recv_sem=env_recv.at[sector, k],
            device_id={"blk": target},
            device_id_type=MESH,
        )

    reach = (chips - 1) // 2
    halves = (range(CHUNKS // 2), range(CHUNKS // 2, CHUNKS))
    orders = (range(CHUNKS), [(k + CHUNKS // 2) % CHUNKS for k in range(CHUNKS)])

    def comes(distance, k, way):
        there = distance <= reach
        if chips % 2 == 0 and k in halves[way - 1]:
            there = there | (distance == chips // 2)
        return there

    def onward(use, sector, distance, k, way, source=None):
        target = following if way == 1 else previous
        pl.when(jnp.asarray(comes(distance + 1, k, way)))(lambda: use(env_copy(sector, k, way, target, source)))

    def start(copy):
        copy.start()

    def sent_off(copy):
        copy.wait_send()

    late = range(CHUNKS // 2, CHUNKS) if reach == 1 and chips == 4 else range(0)
    span = max(share // 2, 1)

    def held(sector):
        return (sector // 2) // span == group

    def own_toward(use, n):
        for way in (1, 2):
            k = orders[way - 1][n]
            onward(use, me, 0, k, way, right.at[pieces(k), 0])

    for n in range(CHUNKS):
        if n in late:
            pl.when(jnp.logical_not(held(me)))(functools.partial(own_toward, start, n))
        else:
            own_toward(start, n)
        env_copy(me, n, 0, sister, right.at[pieces(n), 0]).start()

    row = lax.broadcasted_iota(jnp.int32, (size, width), 0)
    lane = lax.broadcasted_iota(jnp.int32, (size, width), 1)
    load_left_live.wait()
    load_right_live.wait()
    row_live = row < left_live[me]

    load_psi.wait()
    load_left.wait()
    stacked = left_v[...].reshape(terms * size, size)

    def mix(pair, carry):
        blocks = []
        for half in range(2):
            sector = 2 * pair + half
            block = psi_v[:, pl.ds(pl.multiple_of(sector * width, width), width)].astype(jnp.float32)
            live = row_live & (lane < right_live[sector])
            blocks.append(jnp.where(live, block, 0.0).astype(jnp.bfloat16))
        both = jnp.dot(stacked, jnp.concatenate(blocks, axis=1), preferred_element_type=jnp.float32)
        both = both.astype(jnp.bfloat16)
        for half in range(2):
            mixed[2 * pair + half] = both[:, half * width:(half + 1) * width].reshape(terms, size, width)
        return carry

    lax.fori_loop(0, chips, mix, 0)

    def sum_copy(sector):
        return pltpu.make_async_remote_copy(
            src_ref=sent.at[sector],
            dst_ref=landed.at[group, sector % share],
            send_sem=sum_send.at[sector],
            recv_sem=sum_recv.at[group, sector % share],
            device_id={"ops": sector // share},
            device_id_type=MESH,
        )

    def finish(sector):
        lhs = jnp.concatenate([mixed[sector, w] for w in range(terms)], axis=1)
        rhs = jnp.concatenate([rights[sector, w] for w in range(terms)], axis=1)
        value = lax.dot_general(lhs, rhs, (((1,), (1,)), ((), ())), preferred_element_type=jnp.float32)
        mine = sector // share == group

        @pl.when(mine)
        def _():
            own[sector % share] = value

        @pl.when(jnp.logical_not(mine))
        def _():
            sent[sector] = value.astype(sent.dtype)
            sum_copy(sector).start()

    def arrive(sector):
        for k in range(CHUNKS):
            env_copy(sector, k, 0, sister).wait_recv()

    def at(distance, way, core_of):
        shift = 2 * distance if way == 2 else sectors - 2 * distance
        return (core_of + shift) % sectors

    def relay(distance, n):
        for way in (1, 2):
            k = orders[way - 1][n]
            sector = at(distance, way, me)

            now = comes(distance, k, way)
            if n in late:
                now = now & jnp.logical_not((distance == 1) & held(sector))

            @pl.when(now)
            def _():
                env_copy(sector, k, 0, sister).wait_recv()
                onward(start, sector, distance, k, way)
                env_copy(sector, k, 0, sister).start()

    def finish_sister(sector):
        arrive(sector)
        finish(sector)

    load_right.wait()

    def step(distance, carry):
        behind = distance - 1
        above = (behind > 0) & (2 * behind != chips)
        below = True
        if late:
            below = jnp.logical_not((behind == 1) & held(at(behind, 1, me)))
            above = above & jnp.logical_not((behind == 1) & held(at(behind, 2, me)))
        below = jnp.asarray(below)
        relay(distance, 0)
        pl.when(below)(lambda: finish(at(behind, 1, me)))
        pl.when(above)(lambda: finish(at(behind, 2, me)))
        for n in range(1, CHUNKS):
            if n in late and n - 1 not in late:
                @pl.when((distance == 1) & held(me))
                def _():
                    for m in late:
                        own_toward(start, m)
            relay(distance, n)
        pl.when(below)(lambda: finish_sister(at(behind, 1, sister)))
        pl.when(above)(lambda: finish_sister(at(behind, 2, sister)))
        return carry

    lax.fori_loop(1, chips // 2 + 2, step, 0)

    for way in (1, 2) if late else ():
        sector = at(1, way, me)

        @pl.when(held(sector))
        def _():
            for n in late:
                k = orders[way - 1][n]
                env_copy(sector, k, 0, sister).wait_recv()
                env_copy(sector, k, 0, sister).start()
            finish(sector)
            finish_sister(at(1, way, sister))

    def gather(slot, carry):
        total = own[slot]
        for turn in range(1, groups):
            source = (group + turn) % groups
            pltpu.make_async_remote_copy(
                src_ref=sent.at[slot],
                dst_ref=landed.at[source, slot],
                send_sem=sum_send.at[slot],
                recv_sem=sum_recv.at[source, slot],
                device_id={"ops": source},
                device_id_type=MESH,
            ).wait_recv()
            total = total + landed[source, slot].astype(jnp.float32)
        live = row_live & (lane < right_live[group * share + slot])
        out[:, pl.ds(pl.multiple_of(slot * width, width), width)] = jnp.where(live, total, 0.0)
        return carry

    lax.fori_loop(0, share, gather, 0)

    for n in range(CHUNKS):
        own_toward(sent_off, n)
        env_copy(me, n, 0, sister, right.at[pieces(n), 0]).wait_send()

    def drain_env(distance, carry):
        for way in (1, 2):
            for k in range(CHUNKS):
                sector = at(distance, way, me)

                @pl.when(comes(distance, k, way))
                def _():
                    onward(sent_off, sector, distance, k, way)
                    env_copy(sector, k, 0, sister).wait_send()

        return carry

    lax.fori_loop(1, chips // 2 + 1, drain_env, 0)

    def drain_sums(sector, carry):
        pl.when(sector // share != group)(lambda: sum_copy(sector).wait_send())
        return carry

    lax.fori_loop(0, sectors, drain_sums, 0)


def shards(psi, left_env, right_env, left_live, right_live):
    groups, sectors = lax.axis_size("ops"), lax.axis_size("blk")
    terms, size, width = left_env.shape[0], left_env.shape[2], right_env.shape[2]
    share = sectors // groups
    bf16, f32 = jnp.bfloat16, jnp.float32
    buffers = [
        ((size, sectors * width), bf16),
        ((terms, size, size), bf16),
        ((sectors, terms, size, width), bf16),
        ((sectors, terms, width, width), bf16),
        ((sectors, size, width), bf16),
        ((groups, share, size, width), bf16),
        ((share, size, width), f32),
    ]
    dma = pltpu.SemaphoreType.DMA
    return pl.pallas_call(
        functools.partial(kernel, groups, sectors),
        out_shape=pltpu.VMEM((size, share * width), f32),
        in_specs=[pl.BlockSpec(memory_space=pltpu.HBM)] * 5,
        out_specs=pl.BlockSpec(memory_space=pltpu.VMEM),
        scratch_shapes=[pltpu.SMEM((sectors,), jnp.int32)] * 2 + [pltpu.VMEM(shape, kind) for shape, kind in buffers] + [
            dma((5,)),
            dma((sectors, 3, CHUNKS)),
            dma((sectors, CHUNKS)),
            dma((sectors,)),
            dma((groups, share)),
        ],
        compiler_params=pltpu.CompilerParams(
            collective_id=0, has_side_effects=True,
            vmem_limit_bytes=VMEM,
        ),
    )(left_live, right_live, psi, left_env, right_env)


def solution(mesh):
    in_specs = (P("blk", None), P("ops", "blk", None, None), P("ops", "blk", None, None), P(), P())
    out_specs = P("blk", "ops")
    return jax.shard_map(shards, mesh=mesh, in_specs=in_specs, out_specs=out_specs, check_vma=False)
```

```python
import functools

import jax
import jax.numpy as jnp
from jax import lax
from jax.experimental import pallas as pl
from jax.experimental.pallas import tpu as pltpu
from jax.sharding import PartitionSpec as P

MESH = pl.DeviceIdType.MESH
CHUNKS = 4
VMEM = 60 << 20


def kernel(
    groups, sectors, left_hbm, right_hbm, psi, left, right, out,
    left_live, right_live, psi_v, left_v, mixed, rights, sent, landed, own,
    local_sem, env_send, env_recv, sum_send, sum_recv,
):
    terms, size, width = left.shape[0], left.shape[2], right.shape[2]
    share = sectors // groups
    chips = sectors // 2
    part = terms // CHUNKS
    group, me = lax.axis_index("ops"), lax.axis_index("blk")
    chip, core = me // 2, me % 2
    sister = 2 * chip + 1 - core
    has_prev, has_next = chip > 0, chip < chips - 1

    load_psi = pltpu.make_async_copy(psi, psi_v, local_sem.at[0])
    load_left = pltpu.make_async_copy(left.at[:, 0], left_v, local_sem.at[1])
    load_right = pltpu.make_async_copy(right.at[:, 0], rights.at[me], local_sem.at[2])
    load_left_live = pltpu.make_async_copy(left_hbm, left_live, local_sem.at[3])
    load_right_live = pltpu.make_async_copy(right_hbm, right_live, local_sem.at[4])
    load_left_live.start()
    load_right_live.start()
    load_psi.start()
    load_left.start()
    load_right.start()

    barrier = pltpu.get_barrier_semaphore()

    def greet(where):
        pl.semaphore_signal(barrier, inc=1, device_id=where, device_id_type=MESH)

    greet({"blk": sister})
    pl.when(has_prev)(lambda: greet({"blk": me - 2}))
    pl.when(has_next)(lambda: greet({"blk": me + 2}))
    for step in range(1, groups):
        greet({"ops": (group + step) % groups})
    pl.semaphore_wait(barrier, groups + has_prev.astype(jnp.int32) + has_next.astype(jnp.int32))

    def pieces(k):
        return pl.ds(k * part, part)

    def env_copy(sector, k, way, target, source=None):
        landing = rights.at[sector, pieces(k)]
        return pltpu.make_async_remote_copy(
            src_ref=landing if source is None else source,
            dst_ref=landing,
            send_sem=env_send.at[sector, way, k],
            recv_sem=env_recv.at[sector, k],
            device_id={"blk": target},
            device_id_type=MESH,
        )

    def own_copy(k, way, target):
        return env_copy(me, k, way, target, right.at[pieces(k), 0])

    late = range(CHUNKS - 1, CHUNKS)
    span = max(share // 2, 1)

    def held_group(end, side):
        return jnp.where(group == end // span, jnp.where(side == 0, 1, groups - 2), group)

    def held(end, side, at):
        return (at // span == held_group(end, side)) & (at != end)

    def each_held(end, side, use):
        for n in range(span):
            at = held_group(end, side) * span + n
            pl.when(at != end)(functools.partial(use, 2 * at + side))

    first_end, last_end = 0, chips - 1
    at_first, at_last = chip == first_end, chip == last_end

    def up_now(at, k):
        if k not in late:
            return has_next
        return has_next & jnp.logical_not((chip == last_end - 1) & held(last_end, core, at))

    def down_now(at, k):
        if k not in late:
            return has_prev
        return has_prev & jnp.logical_not((chip == first_end + 1) & held(first_end, core, at))

    for k in range(CHUNKS):
        pl.when(up_now(chip, k))(lambda: own_copy(k, 1, me + 2).start())
        pl.when(down_now(chip, k))(lambda: own_copy(k, 2, me - 2).start())
        own_copy(k, 0, sister).start()

    row = lax.broadcasted_iota(jnp.int32, (size, width), 0)
    lane = lax.broadcasted_iota(jnp.int32, (size, width), 1)
    load_left_live.wait()
    load_right_live.wait()
    row_live = row < left_live[me]

    load_psi.wait()
    load_left.wait()
    stacked = left_v[...].reshape(terms * size, size)

    def mix(pair, carry):
        blocks = []
        for half in range(2):
            sector = 2 * pair + half
            block = psi_v[:, pl.ds(pl.multiple_of(sector * width, width), width)].astype(jnp.float32)
            live = row_live & (lane < right_live[sector])
            blocks.append(jnp.where(live, block, 0.0).astype(jnp.bfloat16))
        both = jnp.dot(stacked, jnp.concatenate(blocks, axis=1), preferred_element_type=jnp.float32)
        both = both.astype(jnp.bfloat16)
        for half in range(2):
            mixed[2 * pair + half] = both[:, half * width:(half + 1) * width].reshape(terms, size, width)
        return carry

    def late_below(side, at):
        return at_last & held(last_end, side, at)

    def late_above(side, at):
        return at_first & held(first_end, side, at)

    def relay(distance, k):
        low, high = me - 2 * distance, me + 2 * distance
        below, above = low >= 0, high < sectors
        if k in late:
            below = below & jnp.logical_not(late_below(core, chip - distance))
            above = above & jnp.logical_not(late_above(core, chip + distance))

        @pl.when(below)
        def _():
            env_copy(low, k, 0, sister).wait_recv()
            pl.when(up_now(chip - distance, k))(lambda: env_copy(low, k, 1, me + 2).start())
            env_copy(low, k, 0, sister).start()

        @pl.when(above)
        def _():
            env_copy(high, k, 0, sister).wait_recv()
            pl.when(down_now(chip + distance, k))(lambda: env_copy(high, k, 2, me - 2).start())
            env_copy(high, k, 0, sister).start()

    lax.fori_loop(0, chips // 2, mix, 0)
    relay(1, 0)
    lax.fori_loop(chips // 2, chips, mix, 0)

    def sum_copy(sector):
        return pltpu.make_async_remote_copy(
            src_ref=sent.at[sector],
            dst_ref=landed.at[group, sector % share],
            send_sem=sum_send.at[sector],
            recv_sem=sum_recv.at[group, sector % share],
            device_id={"ops": sector // share},
            device_id_type=MESH,
        )

    def finish(sector):
        lhs = jnp.concatenate([mixed[sector, w] for w in range(terms)], axis=1)
        rhs = jnp.concatenate([rights[sector, w] for w in range(terms)], axis=1)
        value = lax.dot_general(lhs, rhs, (((1,), (1,)), ((), ())), preferred_element_type=jnp.float32)
        mine = sector // share == group

        @pl.when(mine)
        def _():
            own[sector % share] = value

        @pl.when(jnp.logical_not(mine))
        def _():
            sent[sector] = value.astype(sent.dtype)
            sum_copy(sector).start()

    def arrive(sector):
        for k in range(CHUNKS):
            env_copy(sector, k, 0, sister).wait_recv()

    def finish_sister(sector):
        arrive(sector)
        finish(sector)

    load_right.wait()

    def step(distance, carry):
        behind = distance - 1
        low, high = me - 2 * behind, me + 2 * behind
        below, above = low >= 0, (high < sectors) & (behind > 0)

        def due(side):
            under = below & jnp.logical_not(late_below(side, chip - behind) & (behind > 0))
            return under, above & jnp.logical_not(late_above(side, chip + behind))

        under, over = due(core)
        pl.when(distance > 1)(lambda: relay(distance, 0))
        pl.when(under)(lambda: finish(low))
        pl.when(over)(lambda: finish(high))
        for k in range(1, CHUNKS):
            relay(distance, k)

        @pl.when(distance == max(chips - 2, 1))
        def _():
            def release(way, target, sector):
                for k in late:
                    env_copy(sector, k, way, target).start()

            pl.when(chip == first_end + 1)(lambda: each_held(
                first_end, core, functools.partial(release, 2, me - 2)))
            pl.when(chip == last_end - 1)(lambda: each_held(
                last_end, core, functools.partial(release, 1, me + 2)))

        under, over = due(1 - core)
        pl.when(under)(lambda: finish_sister(sister - 2 * behind))
        pl.when(over)(lambda: finish_sister(sister + 2 * behind))
        return carry

    lax.fori_loop(1, chips + 1, step, 0)

    def take(sector):
        for k in late:
            env_copy(sector, k, 0, sister).wait_recv()
            env_copy(sector, k, 0, sister).start()

    @pl.when(at_first | at_last)
    def _():
        end = jnp.where(at_first, first_end, last_end)
        each_held(end, core, take)
        each_held(end, core, finish)
        each_held(end, 1 - core, finish_sister)

    def gather(slot, carry):
        total = own[slot]
        for turn in range(1, groups):
            source = (group + turn) % groups
            pltpu.make_async_remote_copy(
                src_ref=sent.at[slot],
                dst_ref=landed.at[source, slot],
                send_sem=sum_send.at[slot],
                recv_sem=sum_recv.at[source, slot],
                device_id={"ops": source},
                device_id_type=MESH,
            ).wait_recv()
            total = total + landed[source, slot].astype(jnp.float32)
        live = row_live & (lane < right_live[group * share + slot])
        out[:, pl.ds(pl.multiple_of(slot * width, width), width)] = jnp.where(live, total, 0.0)
        return carry

    lax.fori_loop(0, share, gather, 0)

    for k in range(CHUNKS):
        pl.when(has_next)(lambda: own_copy(k, 1, me + 2).wait_send())
        pl.when(has_prev)(lambda: own_copy(k, 2, me - 2).wait_send())
        own_copy(k, 0, sister).wait_send()

    def drain_env(distance, carry):
        low, high = me - 2 * distance, me + 2 * distance

        @pl.when(low >= 0)
        def _():
            for k in range(CHUNKS):
                pl.when(has_next)(lambda: env_copy(low, k, 1, me + 2).wait_send())
                env_copy(low, k, 0, sister).wait_send()

        @pl.when(high < sectors)
        def _():
            for k in range(CHUNKS):
                pl.when(has_prev)(lambda: env_copy(high, k, 2, me - 2).wait_send())
                env_copy(high, k, 0, sister).wait_send()

        return carry

    lax.fori_loop(1, chips, drain_env, 0)

    def drain_sums(sector, carry):
        pl.when(sector // share != group)(lambda: sum_copy(sector).wait_send())
        return carry

    lax.fori_loop(0, sectors, drain_sums, 0)


def shards(psi, left_env, right_env, left_live, right_live):
    groups, sectors = lax.axis_size("ops"), lax.axis_size("blk")
    terms, size, width = left_env.shape[0], left_env.shape[2], right_env.shape[2]
    share = sectors // groups
    bf16, f32 = jnp.bfloat16, jnp.float32
    buffers = [
        ((size, sectors * width), bf16),
        ((terms, size, size), bf16),
        ((sectors, terms, size, width), bf16),
        ((sectors, terms, width, width), bf16),
        ((sectors, size, width), bf16),
        ((groups, share, size, width), bf16),
        ((share, size, width), f32),
    ]
    dma = pltpu.SemaphoreType.DMA
    return pl.pallas_call(
        functools.partial(kernel, groups, sectors),
        out_shape=pltpu.VMEM((size, share * width), f32),
        in_specs=[pl.BlockSpec(memory_space=pltpu.HBM)] * 5,
        out_specs=pl.BlockSpec(memory_space=pltpu.VMEM),
        scratch_shapes=[pltpu.SMEM((sectors,), jnp.int32)] * 2 + [pltpu.VMEM(shape, kind) for shape, kind in buffers] + [
            dma((5,)),
            dma((sectors, 3, CHUNKS)),
            dma((sectors, CHUNKS)),
            dma((sectors,)),
            dma((groups, share)),
        ],
        compiler_params=pltpu.CompilerParams(
            collective_id=0, has_side_effects=True,
            vmem_limit_bytes=VMEM,
        ),
    )(left_live, right_live, psi, left_env, right_env)


def solution(mesh):
    in_specs = (P("blk", None), P("ops", "blk", None, None), P("ops", "blk", None, None), P(), P())
    out_specs = P("blk", "ops")
    return jax.shard_map(shards, mesh=mesh, in_specs=in_specs, out_specs=out_specs, check_vma=False)
```
